32 devices in a mesh: lat: 8 (over y, x, core), chan: 4 (over z).
Axes of the slice: x: 2, y: 2, z: 4, core: 2. Of those that a mesh axis runs over, the one named last changes fastest.
Arguments:
- grid_field: bfloat16 [8, 2, 384, 1440], P('lat', None, 'chan'), may hold values from -6 to 6
- cotangent: bfloat16 [8, 2, 384, 1440], P('lat', None, 'chan'), may hold values from -6 to 6
- legendre: bfloat16 [40, 1361, 8], P('lat'), may hold values from -1.5 to 1.5
- spectral: float32 [384, 2, 720], P('chan'), may hold values from -3 to 3
- mixing: bfloat16 [384, 384], P(None, 'chan'), may hold values from -0.3125 to 0.3125
- pair_table: int32 [40], replicated, may hold values from 0 to 39, each once
Outputs:
- block_output: bfloat16 [8, 2, 384, 1440], P('lat', None, 'chan')
- grad_input: bfloat16 [8, 2, 384, 1440], P('lat', None, 'chan')
- grad_weights: float32 [384, 2, 720], P('chan')
- grad_mixing: float32 [384, 384], P(None, 'chan')
The draws below stay inside these ranges and needn't reach their ends.
Inputs may be any that keep to these rules, and one draw needn't show every extreme that they name: `pair_table`: each pair p stands for the orders p and 79 - p, whose degree ranges together fill 1361 coefficients. Index i of lat owns the slots i * 5 to (i + 1) * 5 - 1.
All inputs are finite; a program needn't handle non-finite values.
Results may differ from the reference program's by a relative error of at most 0.0067.
Values may be sent and summed in bfloat16 or wider, within the bound.
A program may use at most 128 MiB of HBM per device.

```python
import math
import jax
import jax.numpy as jnp
from jax import lax

C = 384
NLON = 1440
L = 720
MMAX = 80
NP = 8
PL = 1361


def block_levels(own_key, extent, pieces, least, largest):
    def one(dim, shards_of):
        steps = jax.random.uniform(jax.random.fold_in(jax.random.fold_in(own_key, 6), dim), (shards_of,), jnp.float32, least / len(pieces), largest / len(pieces))
        return jnp.repeat(jnp.exp(steps), extent[dim] // shards_of).reshape((-1,) + (1,) * (len(extent) - dim - 1))

    gain = one(*pieces[0])
    for cut in pieces[1:]:
        gain = gain * one(*cut)
    return gain


def bell_draw(key, extent, width, bound, split=(), held_as=jnp.bfloat16):
    array = jax.random.normal(key, extent, jnp.float32) * width
    if len(split) > 0:
        array = block_levels(key, extent, split, -0.22, 0.18) * array
    return jnp.clip(array, min=-bound, max=bound).astype(held_as)


def setup_inputs(seed: int = 0) -> dict:
    key_list = jax.random.split(jax.random.key(seed), 7)
    return {
        "grid_field": bell_draw(key_list[0], (NP, 2, C, NLON), 1.0, 6.0, ((0, 8), (2, 4))),
        "cotangent": bell_draw(key_list[1], (NP, 2, C, NLON), 1.0, 6.0, ((0, 8), (2, 4))),
        "legendre": bell_draw(key_list[2], (MMAX // 2, PL, NP), (2 * NP) ** -0.5, 1.5, ((0, 8),)),
        "spectral": bell_draw(key_list[3], (C, 2, L), 0.5, 3.0, ((0, 4),), jnp.float32),
        "mixing": bell_draw(key_list[4], (C, C), C ** -0.5, 0.3125, ((1, 4),)),
        "pair_table": jax.random.permutation(key_list[5], MMAX // 2).astype(jnp.int32),
    }


def dft_basis(orders):
    lon_index = jnp.arange(NLON, dtype=jnp.int32)
    turns = lon_index[:, None] * orders[None, :] % NLON
    angles = turns.astype(jnp.float32) * (2.0 * math.pi / NLON)
    norm_scale = 1.0 / math.sqrt(NLON)
    basis = jnp.stack([jnp.cos(angles) * norm_scale, -jnp.sin(angles) * norm_scale], axis=1)
    return basis.astype(jnp.bfloat16)

def order_weight(orders):
    return jnp.where(orders == 0, 1.0, 2.0).astype(jnp.float32)

def even_odd(spectrum):
    return jnp.stack([spectrum[:, 0] + spectrum[:, 1], spectrum[:, 0] - spectrum[:, 1]], axis=1).astype(jnp.bfloat16)

def reference(grid_field, cotangent, legendre, spectral, mixing, pair_table):
    orders = jnp.arange(MMAX, dtype=jnp.int32)
    basis = dft_basis(orders).astype(jnp.float32)
    weight_m = order_weight(orders)
    field_wide = grid_field.astype(jnp.float32)
    cot_wide = cotangent.astype(jnp.float32)
    even_x = even_odd(jnp.einsum('khcj,jrm->khcrm', field_wide, basis))
    even_g = even_odd(jnp.einsum('khcj,jrm->khcrm', cot_wide, basis) * weight_m)
    position = jnp.arange(PL, dtype=jnp.int32)
    two_index = jnp.arange(2, dtype=jnp.int32)
    weight_rows = jnp.transpose(spectral, (2, 1, 0))
    weight_pad = jnp.concatenate([weight_rows, jnp.zeros((PL, 2, C), weight_rows.dtype)], axis=0)
    weight_tail = jnp.concatenate([jnp.zeros((L - MMAX + 1, 2, C), weight_rows.dtype), weight_rows], axis=0)

    def slot_step(grad_rows, slot):
        lower = pair_table[slot]
        upper = MMAX - 1 - lower
        leading = position < L - lower
        degree = jnp.where(leading, lower + position, position - (L - MMAX + 1)).astype(jnp.int32)
        order = jnp.where(leading, lower, upper)
        half_pick = jnp.where(leading, 0, 1).astype(jnp.int32)
        parity = (degree + order) % 2
        selector = ((half_pick[:, None, None] == two_index[None, :, None]) & (parity[:, None, None] == two_index[None, None, :])).astype(jnp.float32)
        values = lax.dynamic_index_in_dim(legendre, slot, 0, keepdims=False).astype(jnp.float32)
        columns = jnp.stack([lower, upper]).astype(jnp.int32)
        x_pick = jnp.take(even_x, columns, axis=4).astype(jnp.float32)
        g_pick = jnp.take(even_g, columns, axis=4).astype(jnp.float32)
        coeff_x = lax.optimization_barrier(jnp.sum(jnp.einsum('qk,kecrh->qherc', values, x_pick) * selector[:, :, :, None, None], axis=(1, 2)))
        coeff_g = lax.optimization_barrier(jnp.sum(jnp.einsum('qk,kecrh->qherc', values, g_pick) * selector[:, :, :, None, None], axis=(1, 2)))
        picked = jnp.where(leading[:, None, None], lax.dynamic_slice_in_dim(weight_pad, lower, PL, 0), weight_tail)
        real_w, imag_w = (picked[:, 0], picked[:, 1])
        real_x, imag_x = (coeff_x[:, 0], coeff_x[:, 1])
        real_g, imag_g = (coeff_g[:, 0], coeff_g[:, 1])
        filtered = jnp.stack([real_w * real_x - imag_w * imag_x, real_w * imag_x + imag_w * real_x], axis=1).astype(jnp.bfloat16)
        back_coeff = jnp.stack([real_w * real_g + imag_w * imag_g, real_w * imag_g - imag_w * real_g], axis=1).astype(jnp.bfloat16)
        grad_term = jnp.stack([real_g * real_x + imag_g * imag_x, imag_g * real_x - real_g * imag_x], axis=1)
        grad_rows = grad_rows.at[degree].add(grad_term)

        def synthesize(coeff):
            masked = coeff.astype(jnp.float32)[:, None, None, :, :] * selector[:, :, :, None, None]
            both = jnp.einsum('qk,qherc->kecrh', values, masked)
            return even_odd(both)
        return (grad_rows, (synthesize(filtered), synthesize(back_coeff)))
    grad_rows, (stack_y, stack_dx) = lax.scan(slot_step, jnp.zeros((L, 2, C), jnp.float32), jnp.arange(MMAX // 2, dtype=jnp.int32))
    slot_orders = jnp.stack([pair_table, MMAX - 1 - pair_table], axis=1).reshape(-1)
    basis_slot = dft_basis(slot_orders).astype(jnp.float32)
    weight_slot = order_weight(slot_orders)
    synth_y = jnp.moveaxis(stack_y, 0, 4).reshape(NP, 2, C, 2, MMAX).astype(jnp.float32)
    synth_dx = jnp.moveaxis(stack_dx, 0, 4).reshape(NP, 2, C, 2, MMAX).astype(jnp.float32)
    mixing_wide = mixing.astype(jnp.float32)
    filtered_grid = jnp.einsum('khcrm,jrm->khcj', synth_y * weight_slot, basis_slot)
    skip_path = jnp.einsum('khij,io->khoj', field_wide, mixing_wide)
    block_output = (filtered_grid + skip_path).astype(jnp.bfloat16)
    back_grid = jnp.einsum('khcrm,jrm->khcj', synth_dx, basis_slot)
    back_skip = jnp.einsum('khoj,io->khij', cot_wide, mixing_wide)
    grad_input = (back_grid + back_skip).astype(jnp.bfloat16)
    grad_weights = jnp.transpose(grad_rows, (2, 1, 0)) / math.sqrt(MMAX)
    grad_mixing = jnp.einsum('khij,khoj->io', field_wide, cot_wide) / math.sqrt(2 * NP * NLON)
    return (block_output, grad_input, grad_weights, grad_mixing)
```

```python
import math

import jax
import jax.numpy as jnp
from jax import lax
from jax.sharding import PartitionSpec as P


def dft_basis(orders, longitudes):
    lon_index = jnp.arange(longitudes, dtype=jnp.int32)
    turns = lon_index[:, None] * orders[None, :] % longitudes
    angles = turns.astype(jnp.float32) * (2.0 * math.pi / longitudes)
    norm_scale = 1.0 / math.sqrt(longitudes)
    basis = jnp.stack([jnp.cos(angles) * norm_scale, -jnp.sin(angles) * norm_scale], axis=1)
    return basis.astype(jnp.bfloat16)


def even_odd(spectrum):
    return jnp.stack(
        [spectrum[:, 0] + spectrum[:, 1], spectrum[:, 0] - spectrum[:, 1]], axis=1
    ).astype(jnp.bfloat16)


def local(grid_field, cotangent, legendre, spectral, mixing, pair_table):
    lat_count = lax.axis_size("lat")
    owned = legendre.shape[0]
    packed = legendre.shape[1]
    npairs = legendre.shape[2]
    degrees = spectral.shape[2]
    chan_width = grid_field.shape[2]
    longitudes = grid_field.shape[3]
    order_count = 2 * owned * lat_count
    slot_orders = jnp.stack([pair_table, order_count - 1 - pair_table], axis=1).reshape(-1)
    basis = dft_basis(slot_orders, longitudes)
    weight_m = jnp.where(slot_orders == 0, 1.0, 2.0).astype(jnp.float32)
    spec_x = jnp.einsum("khcj,jrm->khcrm", grid_field, basis, preferred_element_type=jnp.float32)
    spec_g = (
        jnp.einsum("khcj,jrm->khcrm", cotangent, basis, preferred_element_type=jnp.float32)
        * weight_m
    )
    recv_x, recv_g = (
        lax.all_to_all(even_odd(spec_x), "lat", split_axis=4, concat_axis=0, tiled=True),
        lax.all_to_all(even_odd(spec_g), "lat", split_axis=4, concat_axis=0, tiled=True),
    )
    owner_shape = (npairs, 2, chan_width, 2, owned, 2)
    recv_x = recv_x.reshape(owner_shape)
    recv_g = recv_g.reshape(owner_shape)
    slot_start = lax.axis_index("lat") * owned
    lower = lax.dynamic_slice_in_dim(pair_table, slot_start, owned)
    position = jnp.arange(packed, dtype=jnp.int32)[None, :]
    lower_col = lower[:, None]
    leading = position < degrees - lower_col
    degree = jnp.where(leading, lower_col + position, position - (degrees - order_count + 1))
    order = jnp.where(leading, lower_col, order_count - 1 - lower_col)
    half_pick = jnp.where(leading, 0, 1)
    parity = (degree + order) % 2
    two_index = jnp.arange(2, dtype=jnp.int32)
    selector = (
        (half_pick[:, None, None, :] == two_index[None, :, None, None])
        & (parity[:, None, None, :] == two_index[None, None, :, None])
    ).astype(jnp.float32)

    def analyse(received):
        variants = jnp.einsum(
            "pqk,kecrph->phercq", legendre, received, preferred_element_type=jnp.float32
        )
        return jnp.sum(variants * selector[:, :, :, None, None, :], axis=(1, 2))

    coeff_x = analyse(recv_x)
    coeff_g = analyse(recv_g)
    weight_rows = jnp.transpose(spectral, (1, 0, 2))
    weight_pad = jnp.concatenate(
        [weight_rows, jnp.zeros((2, chan_width, packed), jnp.float32)], axis=2
    )
    weight_tail = jnp.concatenate(
        [jnp.zeros((2, chan_width, degrees - order_count + 1), jnp.float32), weight_rows], axis=2
    )
    picked_lead = jnp.stack(
        [lax.dynamic_slice_in_dim(weight_pad, lower[slot], packed, 2) for slot in range(owned)]
    )
    picked = jnp.where(leading[:, None, None, :], picked_lead, weight_tail[None])
    real_w, imag_w = (picked[:, 0], picked[:, 1])
    real_x, imag_x = (coeff_x[:, 0], coeff_x[:, 1])
    real_g, imag_g = (coeff_g[:, 0], coeff_g[:, 1])
    filtered = jnp.stack(
        [real_w * real_x - imag_w * imag_x, real_w * imag_x + imag_w * real_x], axis=1
    ).astype(jnp.bfloat16)
    back_coeff = jnp.stack(
        [real_w * real_g + imag_w * imag_g, real_w * imag_g - imag_w * real_g], axis=1
    ).astype(jnp.bfloat16)
    grad_term = jnp.stack(
        [real_g * real_x + imag_g * imag_x, imag_g * real_x - real_g * imag_x], axis=1
    )
    grad_rows = jnp.zeros((2, chan_width, degrees + packed), jnp.float32)
    for slot in range(owned):
        head_part = jnp.where(leading[slot][None, None, :], grad_term[slot], 0.0)
        current = lax.dynamic_slice_in_dim(grad_rows, lower[slot], packed, 2)
        grad_rows = lax.dynamic_update_slice_in_dim(grad_rows, current + head_part, lower[slot], 2)
    tail_part = jnp.sum(jnp.where(leading[:, None, None, :], 0.0, grad_term), axis=0)
    grad_local = jnp.transpose(
        grad_rows[:, :, :degrees] + tail_part[:, :, degrees - order_count + 1 :], (1, 0, 2)
    )

    def synthesize(coeff):
        masked = (
            coeff[:, None, None].astype(jnp.float32) * selector[:, :, :, None, None, :]
        ).astype(jnp.bfloat16)
        both = jnp.einsum(
            "pqk,phercq->kecrph", legendre, masked, preferred_element_type=jnp.float32
        )
        return even_odd(both.reshape(npairs, 2, chan_width, 2, 2 * owned))

    row_y, row_dx = (
        lax.all_to_all(synthesize(filtered), "lat", split_axis=0, concat_axis=4, tiled=True),
        lax.all_to_all(synthesize(back_coeff), "lat", split_axis=0, concat_axis=4, tiled=True),
    )
    filtered_grid = jnp.einsum(
        "khcrm,jrm->khcj",
        row_y * weight_m.astype(jnp.bfloat16),
        basis,
        preferred_element_type=jnp.float32,
    )
    back_grid = jnp.einsum("khcrm,jrm->khcj", row_dx, basis, preferred_element_type=jnp.float32)
    field_full, cot_full, mixing_full = (
        lax.all_gather(grid_field, "chan", axis=2, tiled=True),
        lax.all_gather(cotangent, "chan", axis=2, tiled=True),
        lax.all_gather(mixing, "chan", axis=1, tiled=True),
    )
    mixing_own = lax.dynamic_slice_in_dim(
        mixing_full, lax.axis_index("chan") * chan_width, chan_width, 0
    )
    skip_path = jnp.einsum("khij,io->khoj", field_full, mixing, preferred_element_type=jnp.float32)
    back_skip = jnp.einsum(
        "khoj,io->khij", cot_full, mixing_own, preferred_element_type=jnp.float32
    )
    mixing_grad = jnp.einsum(
        "khij,khoj->io", field_full, cotangent, preferred_element_type=jnp.float32
    )
    block_output = (filtered_grid + skip_path).astype(jnp.bfloat16)
    grad_input = (back_grid + back_skip).astype(jnp.bfloat16)
    weight_sum, mixing_sum = lax.psum((grad_local, mixing_grad), "lat")
    grad_weights = weight_sum / math.sqrt(order_count)
    grad_mixing = mixing_sum / math.sqrt(2 * npairs * longitudes)
    return (block_output, grad_input, grad_weights, grad_mixing)


def solution(mesh):
    in_specs = (
        P("lat", None, "chan", None),
        P("lat", None, "chan", None),
        P("lat", None, None),
        P("chan", None, None),
        P(None, "chan"),
        P(),
    )
    out_specs = (
        P("lat", None, "chan", None),
        P("lat", None, "chan", None),
        P("chan", None, None),
        P(None, "chan"),
    )
    return jax.shard_map(local, mesh=mesh, in_specs=in_specs, out_specs=out_specs, check_vma=False)
```

```python
import functools
import math

import jax
import jax.numpy as jnp
from jax import lax
from jax.experimental import pallas as pl
from jax.experimental.pallas import tpu as pltpu
from jax.sharding import PartitionSpec as P


def dft_basis(orders, longitudes):
    lon_index = jnp.arange(longitudes, dtype=jnp.int32)
    turns = orders[:, None] * lon_index[None, :] % longitudes
    angles = turns.astype(jnp.float32) * (2.0 * math.pi / longitudes)
    norm_scale = 1.0 / math.sqrt(longitudes)
    basis = jnp.stack([jnp.cos(angles) * norm_scale, -jnp.sin(angles) * norm_scale], axis=0)
    return basis.astype(jnp.bfloat16)


def owner_kernel(
    degrees, tail_shift, chunk, lower_ref, leg_ref, recv_ref, lead_ref, tail_ref,
    synth_ref, grad_ref, coeff_ref, head_acc, tail_acc,
):
    slot = pl.program_id(0)
    lower = lower_ref[slot]
    qpad = leg_ref.shape[2]
    half_rows = leg_ref.shape[1] // 2

    @pl.when(slot == 0)
    def _():
        head_acc[...] = jnp.zeros_like(head_acc)
        tail_acc[...] = jnp.zeros_like(tail_acc)

    for start in range(0, qpad, chunk):
        rows = pl.ds(start, chunk)
        leg_t = leg_ref[0, :, start : start + chunk].astype(jnp.float32).T.astype(jnp.bfloat16)

        def analyse(part):
            return jnp.dot(leg_t, recv_ref[0, part], preferred_element_type=jnp.float32)

        x0, x1, g0, g1 = [analyse(part) for part in range(4)]
        position = start + lax.broadcasted_iota(jnp.int32, x0.shape, 0)
        leading = position < degrees - lower
        lead_rows = pl.ds(lower + start, chunk)
        w0 = jnp.where(leading, lead_ref[0, lead_rows, :], tail_ref[0, rows, :])
        w1 = jnp.where(leading, lead_ref[1, lead_rows, :], tail_ref[1, rows, :])
        coeff_ref[0, rows, :] = (w0 * x0 - w1 * x1).astype(jnp.bfloat16)
        coeff_ref[1, rows, :] = (w0 * x1 + w1 * x0).astype(jnp.bfloat16)
        coeff_ref[2, rows, :] = (w0 * g0 + w1 * g1).astype(jnp.bfloat16)
        coeff_ref[3, rows, :] = (w0 * g1 - w1 * g0).astype(jnp.bfloat16)
        for part, term in enumerate((g0 * x0 + g1 * x1, g1 * x0 - g0 * x1)):
            head_acc[part, lead_rows, :] += jnp.where(leading, term, 0.0)
            tail_acc[part, rows, :] += jnp.where(leading, 0.0, term)

    for part in range(4):
        both = jnp.dot(leg_ref[0], coeff_ref[part], preferred_element_type=jnp.float32)
        even, odd = both[:half_rows], both[half_rows:]
        synth_ref[0, part, :half_rows] = (even + odd).astype(jnp.bfloat16)
        synth_ref[0, part, half_rows:] = (even - odd).astype(jnp.bfloat16)

    @pl.when(slot == pl.num_programs(0) - 1)
    def _():
        for part in range(2):
            grad_ref[part] = (
                head_acc[part, :degrees, :] + tail_acc[part, tail_shift : tail_shift + degrees, :]
            )


def owner_stage(lower, leg_masked, received, spectral, order_count):
    owned, rows, qpad = leg_masked.shape
    width = received.shape[3]
    degrees = spectral.shape[2]
    tail_shift = degrees - order_count + 1
    weight_rows = jnp.transpose(spectral, (1, 2, 0))
    lead = jnp.pad(weight_rows, ((0, 0), (0, qpad), (0, 0)))
    tail = jnp.pad(weight_rows, ((0, 0), (tail_shift, qpad - tail_shift - degrees), (0, 0)))
    per_slot = lambda s: (s, 0, 0)
    return pl.pallas_call(
        functools.partial(owner_kernel, degrees, tail_shift, 128),
        grid=(owned,),
        out_shape=(
            jax.ShapeDtypeStruct((owned, 4, rows, width), jnp.bfloat16),
            jax.ShapeDtypeStruct((2, degrees, width), jnp.float32),
        ),
        in_specs=[
            pl.BlockSpec(memory_space=pltpu.SMEM),
            pl.BlockSpec((1, rows, qpad), per_slot),
            pl.BlockSpec((1, 4, rows, width), lambda s: (s, 0, 0, 0)),
            pl.BlockSpec(lead.shape, lambda s: (0, 0, 0)),
            pl.BlockSpec(tail.shape, lambda s: (0, 0, 0)),
        ],
        out_specs=(
            pl.BlockSpec((1, 4, rows, width), lambda s: (s, 0, 0, 0)),
            pl.BlockSpec((2, degrees, width), lambda s: (0, 0, 0)),
        ),
        scratch_shapes=[
            pltpu.VMEM((4, qpad, width), jnp.bfloat16),
            pltpu.VMEM(lead.shape, jnp.float32),
            pltpu.VMEM(tail.shape, jnp.float32),
        ],
        compiler_params=pltpu.CompilerParams(vmem_limit_bytes=32 * 2**20),
        cost_estimate=pl.CostEstimate(
            flops=owned * 16 * rows * qpad * width, bytes_accessed=2**24, transcendentals=0
        ),
    )(lower, leg_masked, received, lead, tail)


def lat_sum(array):
    lat_count = lax.axis_size("lat")
    groups, rows, columns = array.shape
    share = -(-rows // (8 * lat_count)) * 8
    padded = jnp.pad(array, ((0, 0), (0, share * lat_count - rows), (0, 0)))
    parts = padded.reshape(groups, lat_count, share, columns).transpose(1, 0, 2, 3)
    mine = jnp.sum(lax.all_to_all(parts, "lat", 0, 0, tiled=True), axis=0)
    every = lax.all_to_all(
        jnp.broadcast_to(mine[None], (lat_count, *mine.shape)), "lat", 0, 0, tiled=True
    )
    return every.transpose(1, 0, 2, 3).reshape(groups, -1, columns)[:, :rows]


def local(grid_field, cotangent, legendre, spectral, mixing, pair_table):
    lat_count = lax.axis_size("lat")
    owned, packed, npairs = legendre.shape
    degrees = spectral.shape[2]
    chan_width = grid_field.shape[2]
    longitudes = grid_field.shape[3]
    order_count = 2 * owned * lat_count
    field_full = lax.all_gather(grid_field[0], "chan", axis=0, tiled=False)
    cot_full = lax.all_gather(cotangent[0], "chan", axis=0, tiled=False)
    mixing_full = lax.all_gather(mixing, "chan", axis=0, tiled=False)
    slot_orders = jnp.stack([pair_table, order_count - 1 - pair_table], axis=1).reshape(-1)
    basis = dft_basis(slot_orders, longitudes)
    weight_m = jnp.where(slot_orders == 0, 1.0, 2.0).astype(jnp.float32)

    def transform(field):
        spec = jnp.einsum("rmj,hcj->hrmc", basis, field[0], preferred_element_type=jnp.float32)
        return spec

    def parity_parts(spec):
        return jnp.stack([spec[0] + spec[1], spec[0] - spec[1]], axis=0).astype(jnp.bfloat16)

    even_x = parity_parts(transform(grid_field))
    even_g = parity_parts(transform(cotangent) * weight_m[None, None, :, None])
    spectra = jnp.stack([even_x, even_g], axis=0)
    spectra = spectra.reshape(2, 2, 2, lat_count, owned, 2, chan_width)
    sent = jnp.transpose(spectra, (3, 4, 0, 2, 1, 5, 6))
    received = lax.all_to_all(sent, "lat", split_axis=0, concat_axis=0, tiled=True)
    received = jnp.transpose(received, (1, 2, 3, 4, 5, 0, 6)).reshape(
        owned, 4, 4 * npairs, chan_width
    )

    slot_start = lax.axis_index("lat") * owned
    lower = lax.dynamic_slice_in_dim(pair_table, slot_start, owned)
    qpad = -(-packed // 128) * 128
    position = jnp.arange(qpad, dtype=jnp.int32)[None, :]
    lower_col = lower[:, None]
    leading = position < degrees - lower_col
    degree = jnp.where(leading, lower_col + position, position - (degrees - order_count + 1))
    order = jnp.where(leading, lower_col, order_count - 1 - lower_col)
    half_pick = jnp.where(leading, 0, 1)
    parity = (degree + order) % 2
    group = 2 * parity + half_pick
    leg_rows = jnp.pad(
        jnp.transpose(legendre, (0, 2, 1)), ((0, 0), (0, 0), (0, qpad - packed))
    )
    chosen = group[:, None, None, :] == jnp.arange(4, dtype=jnp.int32)[None, :, None, None]
    leg_masked = jnp.where(chosen, leg_rows[:, None], jnp.zeros((), jnp.bfloat16)).reshape(
        owned, 4 * npairs, qpad
    )

    synth, grad_local = owner_stage(lower, leg_masked, received, spectral, order_count)
    synth = synth.reshape(owned, 2, 2, 2, 2, npairs, chan_width)
    back = jnp.transpose(synth, (5, 0, 1, 2, 3, 4, 6))
    rows = lax.all_to_all(back, "lat", split_axis=0, concat_axis=0, tiled=True)
    rows = jnp.transpose(rows, (2, 4, 3, 0, 1, 5, 6)).reshape(
        2, 2, 2, order_count, chan_width
    )
    row_y = rows[0] * weight_m.astype(jnp.bfloat16)[None, None, :, None]
    row_dx = rows[1]
    weight_sum = lat_sum(grad_local)

    filtered_grid = jnp.einsum(
        "hrmc,rmj->hcj", row_y, basis, preferred_element_type=jnp.float32
    )
    back_grid = jnp.einsum("hrmc,rmj->hcj", row_dx, basis, preferred_element_type=jnp.float32)
    chan_count = lax.axis_size("chan")
    mixing_own = lax.dynamic_slice_in_dim(
        mixing_full, lax.axis_index("chan") * chan_width, chan_width, 1
    )
    mixing_parts = mixing.reshape(chan_count, chan_width, chan_width)
    skip_path = jnp.einsum(
        "zhij,zio->hoj", field_full, mixing_parts, preferred_element_type=jnp.float32
    )
    back_skip = jnp.einsum(
        "zhoj,zio->hij", cot_full, mixing_own, preferred_element_type=jnp.float32
    )
    mixing_grad = jnp.einsum(
        "zhij,hoj->zio", field_full, cotangent[0], preferred_element_type=jnp.float32
    ).reshape(1, chan_count * chan_width, chan_width)
    block_output = (filtered_grid + skip_path).astype(jnp.bfloat16)[None]
    grad_input = (back_grid + back_skip).astype(jnp.bfloat16)[None]
    mixing_sum = lat_sum(mixing_grad)[0]
    grad_weights = jnp.transpose(weight_sum, (2, 0, 1)) / math.sqrt(order_count)
    grad_mixing = mixing_sum / math.sqrt(2 * npairs * longitudes)
    return (block_output, grad_input, grad_weights, grad_mixing)


def solution(mesh):
    in_specs = (
        P("lat", None, "chan", None),
        P("lat", None, "chan", None),
        P("lat", None, None),
        P("chan", None, None),
        P(None, "chan"),
        P(),
    )
    out_specs = (
        P("lat", None, "chan", None),
        P("lat", None, "chan", None),
        P("chan", None, None),
        P(None, "chan"),
    )
    return jax.shard_map(local, mesh=mesh, in_specs=in_specs, out_specs=out_specs, check_vma=False)
```

```python
import functools
import math

import jax
import jax.numpy as jnp
from jax import lax
from jax.experimental import pallas as pl
from jax.experimental.pallas import tpu as pltpu
from jax.sharding import PartitionSpec as P


def dft_basis(orders, longitudes):
    lon_index = jnp.arange(longitudes, dtype=jnp.int32)
    turns = orders[:, None] * lon_index[None, :] % longitudes
    angles = turns.astype(jnp.float32) * (2.0 * math.pi / longitudes)
    norm_scale = 1.0 / math.sqrt(longitudes)
    basis = jnp.stack([jnp.cos(angles) * norm_scale, -jnp.sin(angles) * norm_scale], axis=0)
    return basis.astype(jnp.bfloat16)


def owner_kernel(
    degrees, tail_shift, chunk, lower_ref, leg_ref, recv_ref, lead_ref, tail_ref,
    synth_ref, grad_ref, coeff_ref, head_acc, tail_acc,
):
    slot = pl.program_id(0)
    lower = lower_ref[slot]
    qpad = leg_ref.shape[2]
    half_rows = leg_ref.shape[1] // 2

    @pl.when(slot == 0)
    def _():
        head_acc[...] = jnp.zeros_like(head_acc)
        tail_acc[...] = jnp.zeros_like(tail_acc)

    for start in range(0, qpad, chunk):
        rows = pl.ds(start, chunk)
        leg_t = leg_ref[0, :, start : start + chunk].astype(jnp.float32).T.astype(jnp.bfloat16)

        def analyse(part):
            return jnp.dot(leg_t, recv_ref[0, part], preferred_element_type=jnp.float32)

        x0, x1, g0, g1 = [analyse(part) for part in range(4)]
        position = start + lax.broadcasted_iota(jnp.int32, x0.shape, 0)
        leading = position < degrees - lower
        lead_rows = pl.ds(lower + start, chunk)
        w0 = jnp.where(leading, lead_ref[0, lead_rows, :], tail_ref[0, rows, :])
        w1 = jnp.where(leading, lead_ref[1, lead_rows, :], tail_ref[1, rows, :])
        coeff_ref[0, rows, :] = (w0 * x0 - w1 * x1).astype(jnp.bfloat16)
        coeff_ref[1, rows, :] = (w0 * x1 + w1 * x0).astype(jnp.bfloat16)
        coeff_ref[2, rows, :] = (w0 * g0 + w1 * g1).astype(jnp.bfloat16)
        coeff_ref[3, rows, :] = (w0 * g1 - w1 * g0).astype(jnp.bfloat16)
        for part, term in enumerate((g0 * x0 + g1 * x1, g1 * x0 - g0 * x1)):
            head_acc[part, lead_rows, :] += jnp.where(leading, term, 0.0)
            tail_acc[part, rows, :] += jnp.where(leading, 0.0, term)

    for part in range(4):
        both = jnp.dot(leg_ref[0], coeff_ref[part], preferred_element_type=jnp.float32)
        even, odd = both[:half_rows], both[half_rows:]
        synth_ref[0, part, :half_rows] = (even + odd).astype(jnp.bfloat16)
        synth_ref[0, part, half_rows:] = (even - odd).astype(jnp.bfloat16)

    @pl.when(slot == pl.num_programs(0) - 1)
    def _():
        for part in range(2):
            grad_ref[part] = (
                head_acc[part, :degrees, :] + tail_acc[part, tail_shift : tail_shift + degrees, :]
            )


def owner_stage(lower, leg_masked, received, spectral, order_count):
    owned, rows, qpad = leg_masked.shape
    width = received.shape[3]
    degrees = spectral.shape[2]
    tail_shift = degrees - order_count + 1
    weight_rows = jnp.transpose(spectral, (1, 2, 0))
    lead = jnp.pad(weight_rows, ((0, 0), (0, qpad), (0, 0)))
    tail = jnp.pad(weight_rows, ((0, 0), (tail_shift, qpad - tail_shift - degrees), (0, 0)))
    per_slot = lambda s: (s, 0, 0)
    return pl.pallas_call(
        functools.partial(owner_kernel, degrees, tail_shift, 128),
        grid=(owned,),
        out_shape=(
            jax.ShapeDtypeStruct((owned, 4, rows, width), jnp.bfloat16),
            jax.ShapeDtypeStruct((2, degrees, width), jnp.float32),
        ),
        in_specs=[
            pl.BlockSpec(memory_space=pltpu.SMEM),
            pl.BlockSpec((1, rows, qpad), per_slot),
            pl.BlockSpec((1, 4, rows, width), lambda s: (s, 0, 0, 0)),
            pl.BlockSpec(lead.shape, lambda s: (0, 0, 0)),
            pl.BlockSpec(tail.shape, lambda s: (0, 0, 0)),
        ],
        out_specs=(
            pl.BlockSpec((1, 4, rows, width), lambda s: (s, 0, 0, 0)),
            pl.BlockSpec((2, degrees, width), lambda s: (0, 0, 0)),
        ),
        scratch_shapes=[
            pltpu.VMEM((4, qpad, width), jnp.bfloat16),
            pltpu.VMEM(lead.shape, jnp.float32),
            pltpu.VMEM(tail.shape, jnp.float32),
        ],
        compiler_params=pltpu.CompilerParams(vmem_limit_bytes=32 * 2**20),
        cost_estimate=pl.CostEstimate(
            flops=owned * 16 * rows * qpad * width, bytes_accessed=2**24, transcendentals=0
        ),
    )(lower, leg_masked, received, lead, tail)


def exchange(blocks):
    count = lax.axis_size("chan")
    me = lax.axis_index("chan")
    pick = lambda index: lax.dynamic_index_in_dim(blocks, lax.rem(index, count), 0, keepdims=True)
    arrived = [pick(me)]
    for step in range(1, count):
        pairs = [(source, (source - step) % count) for source in range(count)]
        arrived.append(lax.ppermute(pick(me + count - step), "chan", pairs))
    twice = jnp.concatenate(arrived + arrived[:-1], axis=0)
    return lax.dynamic_slice_in_dim(twice, lax.rem(count - me, count), count, 0)


def scattered_rows(array):
    lat_count = lax.axis_size("lat")
    groups, rows, columns = array.shape
    share = -(-rows // (8 * lat_count)) * 8
    padded = jnp.pad(array, ((0, 0), (0, share * lat_count - rows), (0, 0)))
    return padded.reshape(groups, lat_count, share, columns).transpose(1, 0, 2, 3)


def scatter_sum(array, axis):
    return jnp.sum(lax.all_to_all(array, axis, 0, 0, tiled=True), axis=0)


def spread(array, axis):
    everywhere = jnp.broadcast_to(array[None], (lax.axis_size(axis), *array.shape))
    return lax.all_to_all(everywhere, axis, 0, 0, tiled=True)


def joined_rows(shares, rows):
    every = shares.transpose(1, 0, 2, 3)
    return every.reshape(every.shape[0], -1, every.shape[3])[:, :rows]


def local(grid_field, cotangent, legendre, spectral, mixing, pair_table):
    lat_count = lax.axis_size("lat")
    owned, packed, npairs = legendre.shape
    degrees = spectral.shape[2]
    chan_width = grid_field.shape[2]
    longitudes = grid_field.shape[3]
    order_count = 2 * owned * lat_count
    chan_count = lax.axis_size("chan")
    pieces = chan_count // 2
    span = longitudes // pieces
    both_fields = jnp.stack([grid_field[0], cotangent[0]], axis=0)
    cut = both_fields.reshape(2, 2, chan_width, pieces, span).transpose(1, 3, 0, 2, 4)
    sliced = exchange(cut.reshape(chan_count, 2, chan_width, span))
    mixing_blocks = exchange(jnp.broadcast_to(mixing[None], (chan_count, *mixing.shape)))
    mixing_full = mixing_blocks.transpose(1, 0, 2).reshape(mixing.shape[0], -1)
    slot_orders = jnp.stack([pair_table, order_count - 1 - pair_table], axis=1).reshape(-1)
    basis = dft_basis(slot_orders, longitudes)
    weight_m = jnp.where(slot_orders == 0, 1.0, 2.0).astype(jnp.float32)

    def transform(field):
        spec = jnp.einsum("rmj,hcj->hrmc", basis, field[0], preferred_element_type=jnp.float32)
        return spec

    def parity_parts(spec):
        return jnp.stack([spec[0] + spec[1], spec[0] - spec[1]], axis=0).astype(jnp.bfloat16)

    even_x = parity_parts(transform(grid_field))
    even_g = parity_parts(transform(cotangent) * weight_m[None, None, :, None])
    spectra = jnp.stack([even_x, even_g], axis=0)
    spectra = spectra.reshape(2, 2, 2, lat_count, owned, 2, chan_width)
    sent = jnp.transpose(spectra, (3, 4, 0, 2, 1, 5, 6))
    received = lax.all_to_all(sent, "lat", split_axis=0, concat_axis=0, tiled=True)
    received = jnp.transpose(received, (1, 2, 3, 4, 5, 0, 6)).reshape(
        owned, 4, 4 * npairs, chan_width
    )

    slot_start = lax.axis_index("lat") * owned
    lower = lax.dynamic_slice_in_dim(pair_table, slot_start, owned)
    qpad = -(-packed // 128) * 128
    position = jnp.arange(qpad, dtype=jnp.int32)[None, :]
    lower_col = lower[:, None]
    leading = position < degrees - lower_col
    degree = jnp.where(leading, lower_col + position, position - (degrees - order_count + 1))
    order = jnp.where(leading, lower_col, order_count - 1 - lower_col)
    half_pick = jnp.where(leading, 0, 1)
    parity = (degree + order) % 2
    group = 2 * parity + half_pick
    leg_rows = jnp.pad(
        jnp.transpose(legendre, (0, 2, 1)), ((0, 0), (0, 0), (0, qpad - packed))
    )
    chosen = group[:, None, None, :] == jnp.arange(4, dtype=jnp.int32)[None, :, None, None]
    leg_masked = jnp.where(chosen, leg_rows[:, None], jnp.zeros((), jnp.bfloat16)).reshape(
        owned, 4 * npairs, qpad
    )

    synth, grad_local = owner_stage(lower, leg_masked, received, spectral, order_count)
    synth = synth.reshape(owned, 2, 2, 2, 2, npairs, chan_width)
    back = jnp.transpose(synth, (5, 0, 1, 2, 3, 4, 6))
    rows = lax.all_to_all(back, "lat", split_axis=0, concat_axis=0, tiled=True)
    rows = jnp.transpose(rows, (2, 4, 3, 0, 1, 5, 6)).reshape(
        2, 2, 2, order_count, chan_width
    )
    row_y = rows[0] * weight_m.astype(jnp.bfloat16)[None, None, :, None]
    row_dx = rows[1]
    filtered_grid = jnp.einsum(
        "hrmc,rmj->hcj", row_y, basis, preferred_element_type=jnp.float32
    )
    back_grid = jnp.einsum("hrmc,rmj->hcj", row_dx, basis, preferred_element_type=jnp.float32)
    channels = chan_count * chan_width
    field_slice = sliced[:, 0].reshape(channels, span)
    cot_slice = sliced[:, 1].reshape(channels, span)
    mixing_grad = jnp.einsum("ij,oj->io", field_slice, cot_slice, preferred_element_type=jnp.float32)
    skip_slice = jnp.einsum("io,ij->oj", mixing_full, field_slice, preferred_element_type=jnp.float32)
    back_slice = jnp.einsum("io,oj->ij", mixing_full, cot_slice, preferred_element_type=jnp.float32)
    mixed = jnp.stack(
        [
            skip_slice.astype(jnp.bfloat16).reshape(chan_count, chan_width, span),
            back_slice.astype(jnp.bfloat16).reshape(chan_count, chan_width, span),
        ],
        axis=1,
    )
    home = exchange(mixed)
    home = home.reshape(2, pieces, 2, chan_width, span).transpose(2, 0, 3, 1, 4)
    home = home.reshape(2, 2, chan_width, longitudes).astype(jnp.float32)
    block_output = (filtered_grid + home[0]).astype(jnp.bfloat16)[None]
    grad_input = (back_grid + home[1]).astype(jnp.bfloat16)[None]

    mixing_share = scatter_sum(scattered_rows(mixing_grad[None])[:, 0], "lat")
    by_owner = mixing_share.reshape(-1, chan_count, chan_width).transpose(1, 0, 2)
    mixing_share = jnp.sum(exchange(by_owner), axis=0)
    weight_share = scatter_sum(scattered_rows(grad_local), "lat")
    weight_rows = weight_share.shape[1]
    shares = jnp.concatenate([weight_share.reshape(-1, chan_width), mixing_share], axis=0)
    shares = spread(shares, "lat")
    weight_shares = shares[:, : 2 * weight_rows].reshape(-1, 2, weight_rows, chan_width)
    weight_sum = joined_rows(weight_shares, degrees)
    mixing_sum = joined_rows(shares[:, None, 2 * weight_rows :], channels)[0]
    grad_weights = jnp.transpose(weight_sum, (2, 0, 1)) / math.sqrt(order_count)
    grad_mixing = mixing_sum / math.sqrt(2 * npairs * longitudes)
    return (block_output, grad_input, grad_weights, grad_mixing)


def solution(mesh):
    in_specs = (
        P("lat", None, "chan", None),
        P("lat", None, "chan", None),
        P("lat", None, None),
        P("chan", None, None),
        P(None, "chan"),
        P(),
    )
    out_specs = (
        P("lat", None, "chan", None),
        P("lat", None, "chan", None),
        P("chan", None, None),
        P(None, "chan"),
    )
    return jax.shard_map(local, mesh=mesh, in_specs=in_specs, out_specs=out_specs, check_vma=False)
```

```python
import functools
import math

import jax
import jax.numpy as jnp
from jax import lax
from jax.experimental import pallas as pl
from jax.experimental.pallas import tpu as pltpu
from jax.sharding import PartitionSpec as P


def dft_basis(orders, longitudes):
    lon_index = jnp.arange(longitudes, dtype=jnp.int32)
    turns = orders[:, None] * lon_index[None, :] % longitudes
    angles = turns.astype(jnp.float32) * (2.0 * math.pi / longitudes)
    norm_scale = 1.0 / math.sqrt(longitudes)
    basis = jnp.stack([jnp.cos(angles) * norm_scale, -jnp.sin(angles) * norm_scale], axis=0)
    return basis.astype(jnp.bfloat16)


def owner_kernel(
    degrees, tail_shift, chunk, lower_ref, leg_ref, recv_ref, lead_ref, tail_ref,
    synth_ref, grad_ref, coeff_ref, head_acc, tail_acc,
):
    slot = pl.program_id(0)
    lower = lower_ref[slot]
    qpad = leg_ref.shape[2]
    half_rows = leg_ref.shape[1] // 2

    @pl.when(slot == 0)
    def _():
        head_acc[...] = jnp.zeros_like(head_acc)
        tail_acc[...] = jnp.zeros_like(tail_acc)

    for start in range(0, qpad, chunk):
        rows = pl.ds(start, chunk)
        leg_t = leg_ref[0, :, start : start + chunk].astype(jnp.float32).T.astype(jnp.bfloat16)

        def analyse(part):
            return jnp.dot(leg_t, recv_ref[0, part], preferred_element_type=jnp.float32)

        x0, x1, g0, g1 = [analyse(part) for part in range(4)]
        position = start + lax.broadcasted_iota(jnp.int32, x0.shape, 0)
        leading = position < degrees - lower
        lead_rows = pl.ds(lower + start, chunk)
        w0 = jnp.where(leading, lead_ref[0, lead_rows, :], tail_ref[0, rows, :])
        w1 = jnp.where(leading, lead_ref[1, lead_rows, :], tail_ref[1, rows, :])
        coeff_ref[0, rows, :] = (w0 * x0 - w1 * x1).astype(jnp.bfloat16)
        coeff_ref[1, rows, :] = (w0 * x1 + w1 * x0).astype(jnp.bfloat16)
        coeff_ref[2, rows, :] = (w0 * g0 + w1 * g1).astype(jnp.bfloat16)
        coeff_ref[3, rows, :] = (w0 * g1 - w1 * g0).astype(jnp.bfloat16)
        for part, term in enumerate((g0 * x0 + g1 * x1, g1 * x0 - g0 * x1)):
            head_acc[part, lead_rows, :] += jnp.where(leading, term, 0.0)
            tail_acc[part, rows, :] += jnp.where(leading, 0.0, term)

    for part in range(4):
        both = jnp.dot(leg_ref[0], coeff_ref[part], preferred_element_type=jnp.float32)
        even, odd = both[:half_rows], both[half_rows:]
        synth_ref[0, part, :half_rows] = (even + odd).astype(jnp.bfloat16)
        synth_ref[0, part, half_rows:] = (even - odd).astype(jnp.bfloat16)

    @pl.when(slot == pl.num_programs(0) - 1)
    def _():
        for part in range(2):
            grad_ref[part] = (
                head_acc[part, :degrees, :] + tail_acc[part, tail_shift : tail_shift + degrees, :]
            )


def owner_stage(lower, leg_masked, received, spectral, order_count):
    owned, rows, qpad = leg_masked.shape
    width = received.shape[3]
    degrees = spectral.shape[2]
    tail_shift = degrees - order_count + 1
    weight_rows = jnp.transpose(spectral, (1, 2, 0))
    lead = jnp.pad(weight_rows, ((0, 0), (0, qpad), (0, 0)))
    tail = jnp.pad(weight_rows, ((0, 0), (tail_shift, qpad - tail_shift - degrees), (0, 0)))
    per_slot = lambda s: (s, 0, 0)
    return pl.pallas_call(
        functools.partial(owner_kernel, degrees, tail_shift, 128),
        grid=(owned,),
        out_shape=(
            jax.ShapeDtypeStruct((owned, 4, rows, width), jnp.bfloat16),
            jax.ShapeDtypeStruct((2, degrees, width), jnp.float32),
        ),
        in_specs=[
            pl.BlockSpec(memory_space=pltpu.SMEM),
            pl.BlockSpec((1, rows, qpad), per_slot),
            pl.BlockSpec((1, 4, rows, width), lambda s: (s, 0, 0, 0)),
            pl.BlockSpec(lead.shape, lambda s: (0, 0, 0)),
            pl.BlockSpec(tail.shape, lambda s: (0, 0, 0)),
        ],
        out_specs=(
            pl.BlockSpec((1, 4, rows, width), lambda s: (s, 0, 0, 0)),
            pl.BlockSpec((2, degrees, width), lambda s: (0, 0, 0)),
        ),
        scratch_shapes=[
            pltpu.VMEM((4, qpad, width), jnp.bfloat16),
            pltpu.VMEM(lead.shape, jnp.float32),
            pltpu.VMEM(tail.shape, jnp.float32),
        ],
        compiler_params=pltpu.CompilerParams(vmem_limit_bytes=32 * 2**20),
        cost_estimate=pl.CostEstimate(
            flops=owned * 16 * rows * qpad * width, bytes_accessed=2**24, transcendentals=0
        ),
    )(lower, leg_masked, received, lead, tail)


def arrivals(pick):
    count = lax.axis_size("chan")
    me = lax.axis_index("chan")
    arrived = [pick(me, 0)]
    for step in range(1, count):
        pairs = [(source, (source - step) % count) for source in range(count)]
        arrived.append(lax.ppermute(pick(lax.rem(me + count - step, count), step), "chan", pairs))
    return arrived


def mix_kernel(count, me_ref, *refs):
    fields, mixings = refs[:count], refs[count : 2 * count]
    sends, grad_ref = refs[2 * count : 3 * count], refs[3 * count]
    placed, placed_mix, mixed = refs[3 * count + 1 :]
    width = fields[0].shape[1]
    me = me_ref[0]
    for step in range(count):
        rows = pl.ds(pl.multiple_of(lax.rem(me + step, count) * width, 8), width)
        for part in range(2):
            placed[part, rows, :] = fields[step][part].astype(jnp.float32)
        placed_mix[rows, :] = mixings[step][...].astype(jnp.float32)
    field = placed[0].astype(jnp.bfloat16)
    cot = placed[1].astype(jnp.bfloat16)
    mix_t = placed_mix[...]
    mixed[0] = jnp.dot(mix_t.astype(jnp.bfloat16), field, preferred_element_type=jnp.float32)
    mixed[1] = jnp.dot(mix_t.T.astype(jnp.bfloat16), cot, preferred_element_type=jnp.float32)
    grad_ref[...] = lax.dot_general(
        field, cot, (((1,), (1,)), ((), ())), preferred_element_type=jnp.float32
    )
    for step in range(count):
        rows = pl.ds(pl.multiple_of(lax.rem(me + count - step, count) * width, 8), width)
        for part in range(2):
            sends[step][part] = mixed[part, rows, :].astype(jnp.bfloat16)


def mix_stage(me, fields, mixings):
    count = len(fields)
    block = fields[0].shape
    width, span = block[1:]
    channels = count * width
    whole = pl.BlockSpec(memory_space=pltpu.VMEM)
    return pl.pallas_call(
        functools.partial(mix_kernel, count),
        out_shape=tuple(jax.ShapeDtypeStruct(block, jnp.bfloat16) for _ in range(count))
        + (jax.ShapeDtypeStruct((channels, channels), jnp.float32),),
        in_specs=[pl.BlockSpec(memory_space=pltpu.SMEM)] + [whole] * (2 * count),
        out_specs=(whole,) * (count + 1),
        scratch_shapes=[
            pltpu.VMEM((2, channels, span), jnp.float32),
            pltpu.VMEM((channels, channels), jnp.float32),
            pltpu.VMEM((2, channels, span), jnp.float32),
        ],
        compiler_params=pltpu.CompilerParams(vmem_limit_bytes=40 * 2**20),
        cost_estimate=pl.CostEstimate(
            flops=6 * channels * channels * span, bytes_accessed=2**23, transcendentals=0
        ),
    )(me[None], *fields, *mixings)


def output_kernel(count, me_ref, rows_ref, basis_ref, *refs):
    homes, outs, placed = refs[:count], refs[count : count + 2], refs[count + 2]
    pieces = count // 2
    me = me_ref[0]
    for step in range(count):
        placed[lax.rem(me + step, count)] = homes[step][...]
    for part in range(2):
        for half in range(2):
            rows = rows_ref[part, half].astype(jnp.float32).T.astype(jnp.bfloat16)
            grid = jnp.dot(rows, basis_ref[...], preferred_element_type=jnp.float32)
            skip = jnp.concatenate(
                [placed[half * pieces + p, part].astype(jnp.float32) for p in range(pieces)], axis=1
            )
            outs[part][0, half] = (grid + skip).astype(jnp.bfloat16)


def output_stage(me, rows, basis, homes):
    count = len(homes)
    width = rows.shape[3]
    longitudes = basis.shape[1]
    whole = pl.BlockSpec(memory_space=pltpu.VMEM)
    out = jax.ShapeDtypeStruct((1, 2, width, longitudes), jnp.bfloat16)
    return pl.pallas_call(
        functools.partial(output_kernel, count),
        out_shape=(out, out),
        in_specs=[pl.BlockSpec(memory_space=pltpu.SMEM)] + [whole] * (2 + count),
        out_specs=(whole, whole),
        scratch_shapes=[pltpu.VMEM((count, *homes[0].shape), jnp.bfloat16)],
        compiler_params=pltpu.CompilerParams(vmem_limit_bytes=40 * 2**20),
        cost_estimate=pl.CostEstimate(
            flops=8 * rows.shape[2] * width * longitudes, bytes_accessed=2**22, transcendentals=0
        ),
    )(me[None], rows, basis, *homes)


def scattered_rows(array):
    lat_count = lax.axis_size("lat")
    groups, rows, columns = array.shape
    share = -(-rows // (8 * lat_count)) * 8
    padded = jnp.pad(array, ((0, 0), (0, share * lat_count - rows), (0, 0)))
    return padded.reshape(groups, lat_count, share, columns).transpose(1, 0, 2, 3)


def scatter_sum(array, axis):
    return jnp.sum(lax.all_to_all(array, axis, 0, 0, tiled=True), axis=0)


def spread(array, axis):
    everywhere = jnp.broadcast_to(array[None], (lax.axis_size(axis), *array.shape))
    return lax.all_to_all(everywhere, axis, 0, 0, tiled=True)


def joined_rows(shares, rows):
    every = shares.transpose(1, 0, 2, 3)
    return every.reshape(every.shape[0], -1, every.shape[3])[:, :rows]


def local(grid_field, cotangent, legendre, spectral, mixing, pair_table):
    lat_count = lax.axis_size("lat")
    owned, packed, npairs = legendre.shape
    degrees = spectral.shape[2]
    chan_width = grid_field.shape[2]
    longitudes = grid_field.shape[3]
    order_count = 2 * owned * lat_count
    chan_count = lax.axis_size("chan")
    pieces = chan_count // 2
    span = longitudes // pieces
    me = lax.axis_index("chan")
    both_fields = jnp.stack([grid_field[0], cotangent[0]], axis=0)
    cut = both_fields.reshape(2, 2, chan_width, pieces, span).transpose(1, 3, 0, 2, 4)
    cut = cut.reshape(chan_count, 2, chan_width, span)
    field_blocks = arrivals(
        lambda owner, step: lax.dynamic_index_in_dim(cut, owner, 0, keepdims=False)
    )
    mixing_t = mixing.T
    mixing_blocks = arrivals(lambda owner, step: mixing_t)
    *sends, mixing_grad = mix_stage(me, field_blocks, mixing_blocks)
    homes = arrivals(lambda owner, step: sends[step])
    slot_orders = jnp.stack([pair_table, order_count - 1 - pair_table], axis=1).reshape(-1)
    basis = dft_basis(slot_orders, longitudes)
    weight_m = jnp.where(slot_orders == 0, 1.0, 2.0).astype(jnp.float32)

    def transform(field):
        spec = jnp.einsum("rmj,hcj->hrmc", basis, field[0], preferred_element_type=jnp.float32)
        return spec

    def parity_parts(spec):
        return jnp.stack([spec[0] + spec[1], spec[0] - spec[1]], axis=0).astype(jnp.bfloat16)

    even_x = parity_parts(transform(grid_field))
    even_g = parity_parts(transform(cotangent) * weight_m[None, None, :, None])
    spectra = jnp.stack([even_x, even_g], axis=0)
    spectra = spectra.reshape(2, 2, 2, lat_count, owned, 2, chan_width)
    sent = jnp.transpose(spectra, (3, 4, 0, 2, 1, 5, 6))
    received = lax.all_to_all(sent, "lat", split_axis=0, concat_axis=0, tiled=True)
    received = jnp.transpose(received, (1, 2, 3, 4, 5, 0, 6)).reshape(
        owned, 4, 4 * npairs, chan_width
    )

    slot_start = lax.axis_index("lat") * owned
    lower = lax.dynamic_slice_in_dim(pair_table, slot_start, owned)
    qpad = -(-packed // 128) * 128
    position = jnp.arange(qpad, dtype=jnp.int32)[None, :]
    lower_col = lower[:, None]
    leading = position < degrees - lower_col
    degree = jnp.where(leading, lower_col + position, position - (degrees - order_count + 1))
    order = jnp.where(leading, lower_col, order_count - 1 - lower_col)
    half_pick = jnp.where(leading, 0, 1)
    parity = (degree + order) % 2
    group = 2 * parity + half_pick
    leg_rows = jnp.pad(
        jnp.transpose(legendre, (0, 2, 1)), ((0, 0), (0, 0), (0, qpad - packed))
    )
    chosen = group[:, None, None, :] == jnp.arange(4, dtype=jnp.int32)[None, :, None, None]
    leg_masked = jnp.where(chosen, leg_rows[:, None], jnp.zeros((), jnp.bfloat16)).reshape(
        owned, 4 * npairs, qpad
    )

    synth, grad_local = owner_stage(lower, leg_masked, received, spectral, order_count)
    synth = synth.reshape(owned, 2, 2, 2, 2, npairs, chan_width)
    back = jnp.transpose(synth, (5, 1, 3, 2, 0, 4, 6))
    back = back.reshape(npairs, 2, 2, 4 * owned, chan_width)
    rows = lax.all_to_all(back, "lat", split_axis=0, concat_axis=0, tiled=True)
    rows = jnp.transpose(rows, (1, 2, 0, 3, 4)).reshape(2, 2, 2 * order_count, chan_width)
    by_device = lambda a: a.reshape(2, lat_count, 2 * owned, -1).transpose(1, 0, 2, 3)
    row_scale = by_device(jnp.stack([weight_m, weight_m]).astype(jnp.bfloat16))
    row_scale = row_scale.reshape(2 * order_count, 1)
    rows = jnp.stack([rows[0] * row_scale, rows[1]], axis=0)
    row_basis = by_device(basis).reshape(2 * order_count, longitudes)
    block_output, grad_input = output_stage(me, rows, row_basis, homes)
    channels = chan_count * chan_width

    mixing_share = scatter_sum(scattered_rows(mixing_grad[None])[:, 0], "lat")
    by_owner = mixing_share.reshape(-1, chan_count, chan_width).transpose(1, 0, 2)
    shares = arrivals(
        lambda owner, step: lax.dynamic_index_in_dim(by_owner, owner, 0, keepdims=False)
    )
    mixing_share = functools.reduce(jnp.add, shares)
    weight_share = scatter_sum(scattered_rows(grad_local), "lat")
    weight_rows = weight_share.shape[1]
    shares = jnp.concatenate([weight_share.reshape(-1, chan_width), mixing_share], axis=0)
    shares = spread(shares, "lat")
    weight_shares = shares[:, : 2 * weight_rows].reshape(-1, 2, weight_rows, chan_width)
    weight_sum = joined_rows(weight_shares, degrees)
    mixing_sum = joined_rows(shares[:, None, 2 * weight_rows :], channels)[0]
    grad_weights = jnp.transpose(weight_sum, (2, 0, 1)) / math.sqrt(order_count)
    grad_mixing = mixing_sum / math.sqrt(2 * npairs * longitudes)
    return (block_output, grad_input, grad_weights, grad_mixing)


def solution(mesh):
    in_specs = (
        P("lat", None, "chan", None),
        P("lat", None, "chan", None),
        P("lat", None, None),
        P("chan", None, None),
        P(None, "chan"),
        P(),
    )
    out_specs = (
        P("lat", None, "chan", None),
        P("lat", None, "chan", None),
        P("chan", None, None),
        P(None, "chan"),
    )
    return jax.shard_map(local, mesh=mesh, in_specs=in_specs, out_specs=out_specs, check_vma=False)
```

```python
import functools
import math

import jax
import jax.numpy as jnp
from jax import lax
from jax.experimental import pallas as pl
from jax.experimental.pallas import tpu as pltpu
from jax.sharding import PartitionSpec as P


def dft_basis(orders, longitudes):
    lon_index = jnp.arange(longitudes, dtype=jnp.int32)
    turns = orders[:, None] * lon_index[None, :] % longitudes
    angles = turns.astype(jnp.float32) * (2.0 * math.pi / longitudes)
    norm_scale = 1.0 / math.sqrt(longitudes)
    basis = jnp.stack([jnp.cos(angles) * norm_scale, -jnp.sin(angles) * norm_scale], axis=0)
    return basis.astype(jnp.bfloat16)


def owner_kernel(
    degrees, tail_shift, chunk, lower_ref, leg_ref, recv_ref, lead_ref, tail_ref,
    synth_ref, grad_ref, coeff_ref, head_acc, tail_acc,
):
    slot = pl.program_id(0)
    lower = lower_ref[slot]
    qpad = leg_ref.shape[2]
    half_rows = leg_ref.shape[1] // 2

    @pl.when(slot == 0)
    def _():
        head_acc[...] = jnp.zeros_like(head_acc)
        tail_acc[...] = jnp.zeros_like(tail_acc)

    for start in range(0, qpad, chunk):
        rows = pl.ds(start, chunk)
        leg_t = leg_ref[0, :, start : start + chunk].astype(jnp.float32).T.astype(jnp.bfloat16)

        def analyse(part):
            return jnp.dot(leg_t, recv_ref[0, part], preferred_element_type=jnp.float32)

        x0, x1, g0, g1 = [analyse(part) for part in range(4)]
        position = start + lax.broadcasted_iota(jnp.int32, x0.shape, 0)
        leading = position < degrees - lower
        lead_rows = pl.ds(lower + start, chunk)
        w0 = jnp.where(leading, lead_ref[0, lead_rows, :], tail_ref[0, rows, :])
        w1 = jnp.where(leading, lead_ref[1, lead_rows, :], tail_ref[1, rows, :])
        coeff_ref[0, rows, :] = (w0 * x0 - w1 * x1).astype(jnp.bfloat16)
        coeff_ref[1, rows, :] = (w0 * x1 + w1 * x0).astype(jnp.bfloat16)
        coeff_ref[2, rows, :] = (w0 * g0 + w1 * g1).astype(jnp.bfloat16)
        coeff_ref[3, rows, :] = (w0 * g1 - w1 * g0).astype(jnp.bfloat16)
        for part, term in enumerate((g0 * x0 + g1 * x1, g1 * x0 - g0 * x1)):
            head_acc[part, lead_rows, :] += jnp.where(leading, term, 0.0)
            tail_acc[part, rows, :] += jnp.where(leading, 0.0, term)

    for part in range(4):
        both = jnp.dot(leg_ref[0], coeff_ref[part], preferred_element_type=jnp.float32)
        even, odd = both[:half_rows], both[half_rows:]
        synth_ref[0, part, :half_rows] = (even + odd).astype(jnp.bfloat16)
        synth_ref[0, part, half_rows:] = (even - odd).astype(jnp.bfloat16)

    @pl.when(slot == pl.num_programs(0) - 1)
    def _():
        for part in range(2):
            grad_ref[part] = (
                head_acc[part, :degrees, :] + tail_acc[part, tail_shift : tail_shift + degrees, :]
            )


def owner_stage(lower, leg_masked, received, spectral, order_count):
    owned, rows, qpad = leg_masked.shape
    width = received.shape[3]
    degrees = spectral.shape[2]
    tail_shift = degrees - order_count + 1
    weight_rows = jnp.transpose(spectral, (1, 2, 0))
    lead = jnp.pad(weight_rows, ((0, 0), (0, qpad), (0, 0)))
    tail = jnp.pad(weight_rows, ((0, 0), (tail_shift, qpad - tail_shift - degrees), (0, 0)))
    per_slot = lambda s: (s, 0, 0)
    return pl.pallas_call(
        functools.partial(owner_kernel, degrees, tail_shift, 128),
        grid=(owned,),
        out_shape=(
            jax.ShapeDtypeStruct((owned, 4, rows, width), jnp.bfloat16),
            jax.ShapeDtypeStruct((2, degrees, width), jnp.float32),
        ),
        in_specs=[
            pl.BlockSpec(memory_space=pltpu.SMEM),
            pl.BlockSpec((1, rows, qpad), per_slot),
            pl.BlockSpec((1, 4, rows, width), lambda s: (s, 0, 0, 0)),
            pl.BlockSpec(lead.shape, lambda s: (0, 0, 0)),
            pl.BlockSpec(tail.shape, lambda s: (0, 0, 0)),
        ],
        out_specs=(
            pl.BlockSpec((1, 4, rows, width), lambda s: (s, 0, 0, 0)),
            pl.BlockSpec((2, degrees, width), lambda s: (0, 0, 0)),
        ),
        scratch_shapes=[
            pltpu.VMEM((4, qpad, width), jnp.bfloat16),
            pltpu.VMEM(lead.shape, jnp.float32),
            pltpu.VMEM(tail.shape, jnp.float32),
        ],
        compiler_params=pltpu.CompilerParams(vmem_limit_bytes=32 * 2**20),
        cost_estimate=pl.CostEstimate(flops=1, bytes_accessed=1, transcendentals=0),
    )(lower, leg_masked, received, lead, tail)


def arrivals(pick):
    count = lax.axis_size("chan")
    me = lax.axis_index("chan")
    arrived = [pick(me, 0)]
    for step in range(1, count):
        pairs = [(source, (source - step) % count) for source in range(count)]
        arrived.append(lax.ppermute(pick(lax.rem(me + count - step, count), step), "chan", pairs))
    return arrived


def mix_kernel(count, me_ref, *refs):
    fields, mixings = refs[:count], refs[count : 2 * count]
    sends, grad_ref = refs[2 * count : 3 * count], refs[3 * count]
    placed, placed_mix, mixed = refs[3 * count + 1 :]
    width = fields[0].shape[1]
    me = me_ref[0]
    for step in range(count):
        rows = pl.ds(pl.multiple_of(lax.rem(me + step, count) * width, 8), width)
        for part in range(2):
            placed[part, rows, :] = fields[step][part].astype(jnp.float32)
        placed_mix[rows, :] = mixings[step][...].astype(jnp.float32)
    field = placed[0].astype(jnp.bfloat16)
    cot = placed[1].astype(jnp.bfloat16)
    mix_t = placed_mix[...]
    mixed[0] = jnp.dot(mix_t.astype(jnp.bfloat16), field, preferred_element_type=jnp.float32)
    mixed[1] = jnp.dot(mix_t.T.astype(jnp.bfloat16), cot, preferred_element_type=jnp.float32)
    grad_ref[...] = lax.dot_general(
        field, cot, (((1,), (1,)), ((), ())), preferred_element_type=jnp.float32
    )
    for step in range(count):
        rows = pl.ds(pl.multiple_of(lax.rem(me + count - step, count) * width, 8), width)
        for part in range(2):
            sends[step][part] = mixed[part, rows, :].astype(jnp.bfloat16)


def mix_stage(me, fields, mixings):
    count = len(fields)
    block = fields[0].shape
    width, span = block[1:]
    channels = count * width
    whole = pl.BlockSpec(memory_space=pltpu.VMEM)
    return pl.pallas_call(
        functools.partial(mix_kernel, count),
        out_shape=tuple(jax.ShapeDtypeStruct(block, jnp.bfloat16) for _ in range(count))
        + (jax.ShapeDtypeStruct((channels, channels), jnp.float32),),
        in_specs=[pl.BlockSpec(memory_space=pltpu.SMEM)] + [whole] * (2 * count),
        out_specs=(whole,) * (count + 1),
        scratch_shapes=[
            pltpu.VMEM((2, channels, span), jnp.float32),
            pltpu.VMEM((channels, channels), jnp.float32),
            pltpu.VMEM((2, channels, span), jnp.float32),
        ],
        compiler_params=pltpu.CompilerParams(vmem_limit_bytes=40 * 2**20),
        cost_estimate=pl.CostEstimate(flops=1, bytes_accessed=1, transcendentals=0),
    )(me[None], *fields, *mixings)


def output_kernel(count, me_ref, rows_ref, basis_ref, *refs):
    homes, outs, placed = refs[:count], refs[count : count + 2], refs[count + 2]
    pieces = count // 2
    me = me_ref[0]
    for step in range(count):
        placed[lax.rem(me + step, count)] = homes[step][...]
    for part in range(2):
        for half in range(2):
            rows = rows_ref[part, half].astype(jnp.float32).T.astype(jnp.bfloat16)
            grid = jnp.dot(rows, basis_ref[...], preferred_element_type=jnp.float32)
            skip = jnp.concatenate(
                [placed[half * pieces + p, part].astype(jnp.float32) for p in range(pieces)], axis=1
            )
            outs[part][0, half] = (grid + skip).astype(jnp.bfloat16)


def output_stage(me, rows, basis, homes):
    count = len(homes)
    width = rows.shape[3]
    longitudes = basis.shape[1]
    whole = pl.BlockSpec(memory_space=pltpu.VMEM)
    out = jax.ShapeDtypeStruct((1, 2, width, longitudes), jnp.bfloat16)
    return pl.pallas_call(
        functools.partial(output_kernel, count),
        out_shape=(out, out),
        in_specs=[pl.BlockSpec(memory_space=pltpu.SMEM)] + [whole] * (2 + count),
        out_specs=(whole, whole),
        scratch_shapes=[pltpu.VMEM((count, *homes[0].shape), jnp.bfloat16)],
        compiler_params=pltpu.CompilerParams(vmem_limit_bytes=40 * 2**20),
        cost_estimate=pl.CostEstimate(flops=1, bytes_accessed=1, transcendentals=0),
    )(me[None], rows, basis, *homes)


def scattered_rows(array):
    lat_count = lax.axis_size("lat")
    groups, rows, columns = array.shape
    share = -(-rows // (8 * lat_count)) * 8
    padded = jnp.pad(array, ((0, 0), (0, share * lat_count - rows), (0, 0)))
    return padded.reshape(groups, lat_count, share, columns).transpose(1, 0, 2, 3)


def scatter_sum(array, axis):
    return jnp.sum(lax.all_to_all(array, axis, 0, 0, tiled=True), axis=0)


def spread(array, axis):
    everywhere = jnp.broadcast_to(array[None], (lax.axis_size(axis), *array.shape))
    return lax.all_to_all(everywhere, axis, 0, 0, tiled=True)


def joined_rows(shares, rows):
    every = shares.transpose(1, 0, 2, 3)
    return every.reshape(every.shape[0], -1, every.shape[3])[:, :rows]


def local(grid_field, cotangent, legendre, spectral, mixing, pair_table):
    lat_count = lax.axis_size("lat")
    owned, packed, npairs = legendre.shape
    degrees = spectral.shape[2]
    chan_width = grid_field.shape[2]
    longitudes = grid_field.shape[3]
    order_count = 2 * owned * lat_count
    chan_count = lax.axis_size("chan")
    pieces = chan_count // 2
    span = longitudes // pieces
    me = lax.axis_index("chan")
    both_fields = jnp.stack([grid_field[0], cotangent[0]], axis=0)
    cut = both_fields.reshape(2, 2, chan_width, pieces, span).transpose(1, 3, 0, 2, 4)
    cut = cut.reshape(chan_count, 2, chan_width, span)
    cut, grid_field, cotangent = lax.optimization_barrier((cut, grid_field, cotangent))
    field_blocks = arrivals(
        lambda owner, step: lax.dynamic_index_in_dim(cut, owner, 0, keepdims=False)
    )
    mixing_t = mixing.T
    mixing_blocks = arrivals(lambda owner, step: mixing_t)
    slot_orders = jnp.stack([pair_table, order_count - 1 - pair_table], axis=1).reshape(-1)
    basis = dft_basis(slot_orders, longitudes)
    weight_m = jnp.where(slot_orders == 0, 1.0, 2.0).astype(jnp.float32)

    def transform(field):
        spec = jnp.einsum("rmj,hcj->hrmc", basis, field[0], preferred_element_type=jnp.float32)
        return spec

    def parity_parts(spec):
        return jnp.stack([spec[0] + spec[1], spec[0] - spec[1]], axis=0).astype(jnp.bfloat16)

    even_x = parity_parts(transform(grid_field))
    even_g = parity_parts(transform(cotangent) * weight_m[None, None, :, None])
    spectra = jnp.stack([even_x, even_g], axis=0)
    spectra = spectra.reshape(2, 2, 2, lat_count, owned, 2, chan_width)
    sent = jnp.transpose(spectra, (3, 4, 0, 2, 1, 5, 6))
    received = lax.all_to_all(sent, "lat", split_axis=0, concat_axis=0, tiled=True)
    received = jnp.transpose(received, (1, 2, 3, 4, 5, 0, 6)).reshape(
        owned, 4, 4 * npairs, chan_width
    )

    slot_start = lax.axis_index("lat") * owned
    lower = lax.dynamic_slice_in_dim(pair_table, slot_start, owned)
    qpad = -(-packed // 128) * 128
    position = jnp.arange(qpad, dtype=jnp.int32)[None, :]
    lower_col = lower[:, None]
    leading = position < degrees - lower_col
    degree = jnp.where(leading, lower_col + position, position - (degrees - order_count + 1))
    order = jnp.where(leading, lower_col, order_count - 1 - lower_col)
    half_pick = jnp.where(leading, 0, 1)
    parity = (degree + order) % 2
    group = 2 * parity + half_pick
    leg_rows = jnp.pad(
        jnp.transpose(legendre, (0, 2, 1)), ((0, 0), (0, 0), (0, qpad - packed))
    )
    chosen = group[:, None, None, :] == jnp.arange(4, dtype=jnp.int32)[None, :, None, None]
    leg_masked = jnp.where(chosen, leg_rows[:, None], jnp.zeros((), jnp.bfloat16)).reshape(
        owned, 4 * npairs, qpad
    )

    synth, grad_local = owner_stage(lower, leg_masked, received, spectral, order_count)
    synth, field_blocks = lax.optimization_barrier((synth, field_blocks))
    *sends, mixing_grad = mix_stage(me, field_blocks, mixing_blocks)
    grad_local, synth, mixing_grad, sends = lax.optimization_barrier(
        (grad_local, synth, mixing_grad, sends)
    )
    homes = arrivals(lambda owner, step: sends[step])
    synth = synth.reshape(owned, 2, 2, 2, 2, npairs, chan_width)
    back = jnp.transpose(synth, (5, 1, 3, 2, 0, 4, 6))
    back = back.reshape(npairs, 2, 2, 4 * owned, chan_width)
    rows = lax.all_to_all(back, "lat", split_axis=0, concat_axis=0, tiled=True)
    rows = jnp.transpose(rows, (1, 2, 0, 3, 4)).reshape(2, 2, 2 * order_count, chan_width)
    by_device = lambda a: a.reshape(2, lat_count, 2 * owned, -1).transpose(1, 0, 2, 3)
    row_scale = by_device(jnp.stack([weight_m, weight_m]).astype(jnp.bfloat16))
    row_scale = row_scale.reshape(2 * order_count, 1)
    rows = jnp.stack([rows[0] * row_scale, rows[1]], axis=0)
    row_basis = by_device(basis).reshape(2 * order_count, longitudes)
    channels = chan_count * chan_width

    mixing_share = scatter_sum(scattered_rows(mixing_grad[None])[:, 0], "lat")
    by_owner = mixing_share.reshape(-1, chan_count, chan_width).transpose(1, 0, 2)
    shares = arrivals(
        lambda owner, step: lax.dynamic_index_in_dim(by_owner, owner, 0, keepdims=False)
    )
    mixing_share = functools.reduce(jnp.add, shares)
    weight_share = scatter_sum(scattered_rows(grad_local), "lat")
    weight_rows = weight_share.shape[1]
    shares = jnp.concatenate([weight_share.reshape(-1, chan_width), mixing_share], axis=0)
    shares, homes = lax.optimization_barrier((shares, homes))
    shares = spread(shares, "lat")
    weight_shares = shares[:, : 2 * weight_rows].reshape(-1, 2, weight_rows, chan_width)
    weight_sum = joined_rows(weight_shares, degrees)
    mixing_sum = joined_rows(shares[:, None, 2 * weight_rows :], channels)[0]
    block_output, grad_input = output_stage(me, rows, row_basis, homes)
    grad_weights = jnp.transpose(weight_sum, (2, 0, 1)) / math.sqrt(order_count)
    grad_mixing = mixing_sum / math.sqrt(2 * npairs * longitudes)
    return (block_output, grad_input, grad_weights, grad_mixing)


def solution(mesh):
    in_specs = (
        P("lat", None, "chan", None),
        P("lat", None, "chan", None),
        P("lat", None, None),
        P("chan", None, None),
        P(None, "chan"),
        P(),
    )
    out_specs = (
        P("lat", None, "chan", None),
        P("lat", None, "chan", None),
        P("chan", None, None),
        P(None, "chan"),
    )
    return jax.shard_map(local, mesh=mesh, in_specs=in_specs, out_specs=out_specs, check_vma=False)
```

```python
import functools
import math

import jax
import jax.numpy as jnp
from jax import lax
from jax.experimental import pallas as pl
from jax.experimental.pallas import tpu as pltpu
from jax.sharding import PartitionSpec as P


def dft_basis(orders, longitudes):
    lon_index = jnp.arange(longitudes, dtype=jnp.int32)
    turns = orders[:, None] * lon_index[None, :] % longitudes
    angles = turns.astype(jnp.float32) * (2.0 * math.pi / longitudes)
    norm_scale = 1.0 / math.sqrt(longitudes)
    basis = jnp.stack([jnp.cos(angles) * norm_scale, -jnp.sin(angles) * norm_scale], axis=0)
    return basis.astype(jnp.bfloat16)


def owner_kernel(
    degrees, tail_shift, chunk, lower_ref, leg_ref, recv_ref, lead_ref, tail_ref,
    synth_ref, grad_ref, coeff_ref, head_acc, tail_acc,
):
    slot = pl.program_id(0)
    lower = lower_ref[slot]
    qpad = leg_ref.shape[2]
    half_rows = leg_ref.shape[1] // 2

    @pl.when(slot == 0)
    def _():
        head_acc[...] = jnp.zeros_like(head_acc)
        tail_acc[...] = jnp.zeros_like(tail_acc)

    for start in range(0, qpad, chunk):
        rows = pl.ds(start, chunk)
        leg_t = leg_ref[0, :, start : start + chunk].astype(jnp.float32).T.astype(jnp.bfloat16)

        def analyse(part):
            return jnp.dot(leg_t, recv_ref[0, part], preferred_element_type=jnp.float32)

        x0, x1, g0, g1 = [analyse(part) for part in range(4)]
        position = start + lax.broadcasted_iota(jnp.int32, x0.shape, 0)
        leading = position < degrees - lower
        lead_rows = pl.ds(lower + start, chunk)
        w0 = jnp.where(leading, lead_ref[0, lead_rows, :], tail_ref[0, rows, :])
        w1 = jnp.where(leading, lead_ref[1, lead_rows, :], tail_ref[1, rows, :])
        coeff_ref[0, rows, :] = (w0 * x0 - w1 * x1).astype(jnp.bfloat16)
        coeff_ref[1, rows, :] = (w0 * x1 + w1 * x0).astype(jnp.bfloat16)
        coeff_ref[2, rows, :] = (w0 * g0 + w1 * g1).astype(jnp.bfloat16)
        coeff_ref[3, rows, :] = (w0 * g1 - w1 * g0).astype(jnp.bfloat16)
        for part, term in enumerate((g0 * x0 + g1 * x1, g1 * x0 - g0 * x1)):
            head_acc[part, lead_rows, :] += jnp.where(leading, term, 0.0)
            tail_acc[part, rows, :] += jnp.where(leading, 0.0, term)

    for part in range(4):
        both = jnp.dot(leg_ref[0], coeff_ref[part], preferred_element_type=jnp.float32)
        even, odd = both[:half_rows], both[half_rows:]
        synth_ref[0, part, :half_rows] = (even + odd).astype(jnp.bfloat16)
        synth_ref[0, part, half_rows:] = (even - odd).astype(jnp.bfloat16)

    @pl.when(slot == pl.num_programs(0) - 1)
    def _():
        for part in range(2):
            grad_ref[part] = (
                head_acc[part, :degrees, :] + tail_acc[part, tail_shift : tail_shift + degrees, :]
            )


def owner_stage(lower, leg_masked, received, spectral, order_count):
    owned, rows, qpad = leg_masked.shape
    width = received.shape[3]
    degrees = spectral.shape[2]
    tail_shift = degrees - order_count + 1
    weight_rows = jnp.transpose(spectral, (1, 2, 0))
    lead = jnp.pad(weight_rows, ((0, 0), (0, qpad), (0, 0)))
    tail = jnp.pad(weight_rows, ((0, 0), (tail_shift, qpad - tail_shift - degrees), (0, 0)))
    per_slot = lambda s: (s, 0, 0)
    return pl.pallas_call(
        functools.partial(owner_kernel, degrees, tail_shift, 128),
        grid=(owned,),
        out_shape=(
            jax.ShapeDtypeStruct((owned, 4, rows, width), jnp.bfloat16),
            jax.ShapeDtypeStruct((2, degrees, width), jnp.float32),
        ),
        in_specs=[
            pl.BlockSpec(memory_space=pltpu.SMEM),
            pl.BlockSpec((1, rows, qpad), per_slot),
            pl.BlockSpec((1, 4, rows, width), lambda s: (s, 0, 0, 0)),
            pl.BlockSpec(lead.shape, lambda s: (0, 0, 0)),
            pl.BlockSpec(tail.shape, lambda s: (0, 0, 0)),
        ],
        out_specs=(
            pl.BlockSpec((1, 4, rows, width), lambda s: (s, 0, 0, 0)),
            pl.BlockSpec((2, degrees, width), lambda s: (0, 0, 0)),
        ),
        scratch_shapes=[
            pltpu.VMEM((4, qpad, width), jnp.bfloat16),
            pltpu.VMEM(lead.shape, jnp.float32),
            pltpu.VMEM(tail.shape, jnp.float32),
        ],
        compiler_params=pltpu.CompilerParams(vmem_limit_bytes=32 * 2**20),
        cost_estimate=pl.CostEstimate(
            flops=owned * 16 * rows * qpad * width, bytes_accessed=2**24, transcendentals=0
        ),
    )(lower, leg_masked, received, lead, tail)


def arrivals(pick):
    count = lax.axis_size("chan")
    me = lax.axis_index("chan")
    arrived = [pick(me, 0)]
    for step in range(1, count):
        pairs = [(source, (source - step) % count) for source in range(count)]
        arrived.append(lax.ppermute(pick(lax.rem(me + count - step, count), step), "chan", pairs))
    return arrived


def exchange(blocks):
    count = lax.axis_size("chan")
    me = lax.axis_index("chan")
    pick = lambda index: lax.dynamic_index_in_dim(blocks, lax.rem(index, count), 0, keepdims=True)
    arrived = [pick(me)]
    for step in range(1, count):
        pairs = [(source, (source - step) % count) for source in range(count)]
        arrived.append(lax.ppermute(pick(me + count - step), "chan", pairs))
    twice = jnp.concatenate(arrived + arrived[:-1], axis=0)
    return lax.dynamic_slice_in_dim(twice, lax.rem(count - me, count), count, 0)


def output_kernel(count, me_ref, rows_ref, basis_ref, *refs):
    homes, outs, placed = refs[:count], refs[count : count + 2], refs[count + 2]
    pieces = count // 2
    me = me_ref[0]
    for step in range(count):
        placed[lax.rem(me + step, count)] = homes[step][...]
    for part in range(2):
        for half in range(2):
            rows = rows_ref[part, half].astype(jnp.float32).T.astype(jnp.bfloat16)
            grid = jnp.dot(rows, basis_ref[...], preferred_element_type=jnp.float32)
            skip = jnp.concatenate(
                [placed[half * pieces + p, part].astype(jnp.float32) for p in range(pieces)], axis=1
            )
            outs[part][0, half] = (grid + skip).astype(jnp.bfloat16)


def output_stage(me, rows, basis, homes):
    count = len(homes)
    width = rows.shape[3]
    longitudes = basis.shape[1]
    whole = pl.BlockSpec(memory_space=pltpu.VMEM)
    out = jax.ShapeDtypeStruct((1, 2, width, longitudes), jnp.bfloat16)
    return pl.pallas_call(
        functools.partial(output_kernel, count),
        out_shape=(out, out),
        in_specs=[pl.BlockSpec(memory_space=pltpu.SMEM)] + [whole] * (2 + count),
        out_specs=(whole, whole),
        scratch_shapes=[pltpu.VMEM((count, *homes[0].shape), jnp.bfloat16)],
        compiler_params=pltpu.CompilerParams(vmem_limit_bytes=40 * 2**20),
        cost_estimate=pl.CostEstimate(
            flops=8 * rows.shape[2] * width * longitudes, bytes_accessed=2**22, transcendentals=0
        ),
    )(me[None], rows, basis, *homes)


def scattered_rows(array):
    lat_count = lax.axis_size("lat")
    groups, rows, columns = array.shape
    share = -(-rows // (8 * lat_count)) * 8
    padded = jnp.pad(array, ((0, 0), (0, share * lat_count - rows), (0, 0)))
    return padded.reshape(groups, lat_count, share, columns).transpose(1, 0, 2, 3)


def scatter_sum(array, axis):
    return jnp.sum(lax.all_to_all(array, axis, 0, 0, tiled=True), axis=0)


def spread(array, axis):
    everywhere = jnp.broadcast_to(array[None], (lax.axis_size(axis), *array.shape))
    return lax.all_to_all(everywhere, axis, 0, 0, tiled=True)


def joined_rows(shares, rows):
    every = shares.transpose(1, 0, 2, 3)
    return every.reshape(every.shape[0], -1, every.shape[3])[:, :rows]


def local(grid_field, cotangent, legendre, spectral, mixing, pair_table):
    lat_count = lax.axis_size("lat")
    owned, packed, npairs = legendre.shape
    degrees = spectral.shape[2]
    chan_width = grid_field.shape[2]
    longitudes = grid_field.shape[3]
    order_count = 2 * owned * lat_count
    chan_count = lax.axis_size("chan")
    pieces = chan_count // 2
    span = longitudes // pieces
    me = lax.axis_index("chan")
    both_fields = jnp.stack([grid_field[0], cotangent[0]], axis=0)
    cut = both_fields.reshape(2, 2, chan_width, pieces, span).transpose(1, 3, 0, 2, 4)
    cut = cut.reshape(chan_count, 2, chan_width, span)
    sliced = exchange(cut)
    mixing_blocks = exchange(jnp.broadcast_to(mixing[None], (chan_count, *mixing.shape)))
    mixing_full = mixing_blocks.transpose(1, 0, 2).reshape(mixing.shape[0], -1)
    slot_orders = jnp.stack([pair_table, order_count - 1 - pair_table], axis=1).reshape(-1)
    basis = dft_basis(slot_orders, longitudes)
    weight_m = jnp.where(slot_orders == 0, 1.0, 2.0).astype(jnp.float32)

    def transform(field):
        spec = jnp.einsum("rmj,hcj->hrmc", basis, field[0], preferred_element_type=jnp.float32)
        return spec

    def parity_parts(spec):
        return jnp.stack([spec[0] + spec[1], spec[0] - spec[1]], axis=0).astype(jnp.bfloat16)

    even_x = parity_parts(transform(grid_field))
    even_g = parity_parts(transform(cotangent) * weight_m[None, None, :, None])
    spectra = jnp.stack([even_x, even_g], axis=0)
    spectra = spectra.reshape(2, 2, 2, lat_count, owned, 2, chan_width)
    sent = jnp.transpose(spectra, (3, 4, 0, 2, 1, 5, 6))
    received = lax.all_to_all(sent, "lat", split_axis=0, concat_axis=0, tiled=True)
    received = jnp.transpose(received, (1, 2, 3, 4, 5, 0, 6)).reshape(
        owned, 4, 4 * npairs, chan_width
    )

    slot_start = lax.axis_index("lat") * owned
    lower = lax.dynamic_slice_in_dim(pair_table, slot_start, owned)
    qpad = -(-packed // 128) * 128
    position = jnp.arange(qpad, dtype=jnp.int32)[None, :]
    lower_col = lower[:, None]
    leading = position < degrees - lower_col
    degree = jnp.where(leading, lower_col + position, position - (degrees - order_count + 1))
    order = jnp.where(leading, lower_col, order_count - 1 - lower_col)
    half_pick = jnp.where(leading, 0, 1)
    parity = (degree + order) % 2
    group = 2 * parity + half_pick
    leg_rows = jnp.pad(
        jnp.transpose(legendre, (0, 2, 1)), ((0, 0), (0, 0), (0, qpad - packed))
    )
    chosen = group[:, None, None, :] == jnp.arange(4, dtype=jnp.int32)[None, :, None, None]
    leg_masked = jnp.where(chosen, leg_rows[:, None], jnp.zeros((), jnp.bfloat16)).reshape(
        owned, 4 * npairs, qpad
    )

    synth, grad_local = owner_stage(lower, leg_masked, received, spectral, order_count)
    synth = synth.reshape(owned, 2, 2, 2, 2, npairs, chan_width)
    back = jnp.transpose(synth, (5, 1, 3, 2, 0, 4, 6))
    back = back.reshape(npairs, 2, 2, 4 * owned, chan_width)
    rows = lax.all_to_all(back, "lat", split_axis=0, concat_axis=0, tiled=True)
    rows = jnp.transpose(rows, (1, 2, 0, 3, 4)).reshape(2, 2, 2 * order_count, chan_width)
    by_device = lambda a: a.reshape(2, lat_count, 2 * owned, -1).transpose(1, 0, 2, 3)
    row_scale = by_device(jnp.stack([weight_m, weight_m]).astype(jnp.bfloat16))
    row_scale = row_scale.reshape(2 * order_count, 1)
    rows = jnp.stack([rows[0] * row_scale, rows[1]], axis=0)
    row_basis = by_device(basis).reshape(2 * order_count, longitudes)
    channels = chan_count * chan_width
    field_slice = sliced[:, 0].reshape(channels, span)
    cot_slice = sliced[:, 1].reshape(channels, span)
    skip_slice = jnp.einsum("io,ij->oj", mixing_full, field_slice, preferred_element_type=jnp.float32)
    back_slice = jnp.einsum("io,oj->ij", mixing_full, cot_slice, preferred_element_type=jnp.float32)
    mixed = jnp.stack(
        [
            skip_slice.astype(jnp.bfloat16).reshape(chan_count, chan_width, span),
            back_slice.astype(jnp.bfloat16).reshape(chan_count, chan_width, span),
        ],
        axis=1,
    )
    mixed, grad_local, field_slice = lax.optimization_barrier((mixed, grad_local, field_slice))
    mixing_grad = jnp.einsum("ij,oj->io", field_slice, cot_slice, preferred_element_type=jnp.float32)
    homes = arrivals(
        lambda owner, step: lax.dynamic_index_in_dim(mixed, owner, 0, keepdims=False)
    )
    mixing_share = scatter_sum(scattered_rows(mixing_grad[None])[:, 0], "lat")
    by_owner = mixing_share.reshape(-1, chan_count, chan_width).transpose(1, 0, 2)
    shares = arrivals(
        lambda owner, step: lax.dynamic_index_in_dim(by_owner, owner, 0, keepdims=False)
    )
    mixing_share = functools.reduce(jnp.add, shares)
    weight_share = scatter_sum(scattered_rows(grad_local), "lat")
    weight_rows = weight_share.shape[1]
    shares = jnp.concatenate([weight_share.reshape(-1, chan_width), mixing_share], axis=0)
    shares, homes = lax.optimization_barrier((shares, homes))
    shares = spread(shares, "lat")
    weight_shares = shares[:, : 2 * weight_rows].reshape(-1, 2, weight_rows, chan_width)
    weight_sum = joined_rows(weight_shares, degrees)
    mixing_sum = joined_rows(shares[:, None, 2 * weight_rows :], channels)[0]
    block_output, grad_input = output_stage(me, rows, row_basis, homes)
    grad_weights = jnp.transpose(weight_sum, (2, 0, 1)) / math.sqrt(order_count)
    grad_mixing = mixing_sum / math.sqrt(2 * npairs * longitudes)
    return (block_output, grad_input, grad_weights, grad_mixing)


def solution(mesh):
    in_specs = (
        P("lat", None, "chan", None),
        P("lat", None, "chan", None),
        P("lat", None, None),
        P("chan", None, None),
        P(None, "chan"),
        P(),
    )
    out_specs = (
        P("lat", None, "chan", None),
        P("lat", None, "chan", None),
        P("chan", None, None),
        P(None, "chan"),
    )
    return jax.shard_map(local, mesh=mesh, in_specs=in_specs, out_specs=out_specs, check_vma=False)
```
